32 devices in a mesh: clips: 2 (over y), tm: 4 (over z), height: 4 (over x, core).
Axes of the slice: x: 2, y: 2, z: 4, core: 2. Of those that a mesh axis runs over, the one named last changes fastest.
Arguments:
- clip_frames: bfloat16 [32, 32, 16, 192], P(('clips', 'tm'), 'height'), parts along dimension 0, may hold values from -6 to 6
- w_first: bfloat16 [3, 3, 3, 192, 192], replicated, may hold values from -0.078125 to 0.078125
- b_first: float32 [192], replicated, may hold values from -3 to 3
- w_second: bfloat16 [3, 3, 3, 192, 192], replicated, may hold values from -0.078125 to 0.078125
- b_second: float32 [192], replicated, may hold values from -3 to 3
Outputs:
- block_out: bfloat16 [32, 32, 16, 192], P(('clips', 'tm'), 'height'), parts along dimension 0
The draws below stay inside these ranges and needn't reach their ends.
There are 2 independent parts, one for each index of `clips`. The reference program is written for one: setup_inputs(seed, part) draws one part's arguments, and reference() takes and returns one part's arrays. A program takes and returns all parts, laid end to end along the dimension named above; an argument that names none is the same for every part. Nothing has to cross between parts.
All inputs are finite; a program needn't handle non-finite values.
Results may differ from the reference program's by a relative error of at most 0.003.
Values may be sent and summed in bfloat16 or wider, within the bound.
A program may use at most 64 MiB of HBM per device.

```python
import jax
import jax.numpy as jnp
from jax import lax

C = 192
COLS = 16
FRAMES = 16
ROWS = 32


def shard_levels(key, dims, cuts, low, high):
    level = 1.0
    for position, parts in cuts:
        heights = jax.random.uniform(jax.random.fold_in(jax.random.fold_in(key, 6), position), (parts,), jnp.float32, low / len(cuts), high / len(cuts))
        level = level * jnp.repeat(jnp.exp(heights), dims[position] // parts).reshape((-1,) + (1,) * (len(dims) - 1 - position))
    return level


def bell_draw(rng, shape, width, bound, shards=(), kind=jnp.bfloat16):
    drawn = jax.random.normal(rng, shape, jnp.float32) * width
    if len(shards) > 0:
        drawn = shard_levels(rng, shape, shards, -0.22, 0.18) * drawn
    return jnp.clip(drawn, min=-bound, max=bound).astype(kind)


def setup_inputs(seed: int = 0, part: int = 0) -> dict:
    key_list = jax.random.split(jax.random.key(seed), 6)
    own_keys = jax.random.split(jax.random.fold_in(key_list[5], part), 6)
    return {
        "clip_frames": bell_draw(own_keys[0], (FRAMES, ROWS, COLS, C), 1.0, 6.0, ((0, 4), (1, 4))),
        "w_first": bell_draw(key_list[1], (3, 3, 3, C, C), (27 * C) ** -0.5, 0.078125),
        "b_first": bell_draw(key_list[2], (C,), 0.5, 3.0, (), jnp.float32),
        "w_second": bell_draw(key_list[3], (3, 3, 3, C, C), (27 * C) ** -0.5, 0.078125),
        "b_second": bell_draw(key_list[4], (C,), 0.5, 3.0, (), jnp.float32),
    }


def conv_valid(padded, weight):
    frame_count = padded.shape[0] - 2
    row_count = padded.shape[1] - 2
    col_count = padded.shape[2] - 2
    chans = weight.shape[3]
    summed = jnp.zeros((frame_count * row_count * col_count, weight.shape[4]), jnp.float32)
    for tap_time in range(3):
        stacked = jnp.concatenate([padded[tap_time:tap_time + frame_count, tap_row:tap_row + row_count, tap_col:tap_col + col_count] for tap_row in range(3) for tap_col in range(3)], -1)
        stacked = stacked.reshape(-1, 9 * chans)
        kernel = weight[tap_time].reshape(9 * chans, weight.shape[4])
        summed = summed + jnp.dot(stacked, kernel, preferred_element_type=jnp.float32)
    return summed.reshape(frame_count, row_count, col_count, weight.shape[4])


def blocked_conv(field, weight):
    frames = field.shape[0]
    padded = jnp.pad(field, ((2, 0), (1, 1), (1, 1), (0, 0)))
    block_len = 4
    block_count = frames // block_len

    def block_conv(block_index):
        window = lax.dynamic_slice_in_dim(padded, (block_index * block_len).astype(jnp.int32), block_len + 2, 0)
        return conv_valid(window, weight)

    outputs = lax.map(block_conv, jnp.arange(block_count, dtype=jnp.int32))
    return outputs.reshape(frames, field.shape[1], field.shape[2], weight.shape[4])


def reference(clip_frames, w_first, b_first, w_second, b_second):
    activated = jax.nn.silu(clip_frames.astype(jnp.float32)).astype(jnp.bfloat16)
    hidden = blocked_conv(activated, w_first) + b_first
    gated = jax.nn.silu(hidden).astype(jnp.bfloat16)
    second = blocked_conv(gated, w_second) + b_second
    return (clip_frames.astype(jnp.float32) + second).astype(jnp.bfloat16)
```

```python
import functools

import jax
import jax.numpy as jnp
from jax import lax
from jax.experimental import pallas as pl
from jax.experimental.pallas import tpu as pltpu
from jax.sharding import PartitionSpec as P

MESH = pl.DeviceIdType.MESH


def silu(v):
    return 0.5 * v * (1.0 + jnp.tanh(0.5 * v))


def kernel(
    peers_t, peers_h, x_ref, w1_ref, b1_ref, w2_ref, b2_ref, out_ref,
    xbuf, gbuf, stack1, stack2, wv1, wv2, bias, x_sem, b_sem, w_sem, send_sem, recv_sem,
):
    frames, rows, cols, chans = x_ref.shape
    lo_chans = chans - 128
    positions = frames * rows * cols
    depth = stack1.shape[-1]
    tm, height = lax.axis_index("tm"), lax.axis_index("height")
    later, lower, upper = tm < peers_t - 1, height < peers_h - 1, height > 0
    earlier = tm > 0

    every, tail, head = slice(0, frames), slice(frames - 2, frames), slice(0, 2)
    body, first, last = slice(0, rows), slice(0, 1), slice(rows - 1, rows)
    own_f, own_r = slice(2, frames + 2), slice(1, rows + 1)
    above, below = slice(0, 1), slice(rows + 1, rows + 2)
    routes = (
        (1, 0, tail, body, head, own_r, later, earlier),
        (0, 1, every, last, own_f, above, lower, upper),
        (0, -1, every, first, own_f, below, upper, lower),
        (1, 1, tail, last, head, above, later & lower, earlier & upper),
        (1, -1, tail, first, head, below, later & upper, earlier & lower),
    )

    barrier = pltpu.get_barrier_semaphore()
    for dt, dh, _, _, _, _, _, receives in routes:
        @pl.when(receives)
        def _():
            pl.semaphore_signal(
                barrier, inc=1,
                device_id={"tm": jnp.maximum(tm - dt, 0), "height": jnp.clip(height - dh, 0, peers_h - 1)},
                device_id_type=MESH,
            )

    local_x = pltpu.make_async_copy(x_ref, xbuf.at[own_f, own_r], x_sem)
    local_x.start()

    def weight_copies(w_ref, b_ref, wv, which):
        copies = [pltpu.make_async_copy(b_ref, bias.at[which], b_sem.at[which])]
        for a in range(3):
            pairs = [(w_ref.at[a, b, :, 0:2], wv.at[a, 3 * b : 3 * b + 3]) for b in range(3)]
            pairs.append((w_ref.at[a, :, 0:2, 2], wv.at[a, 9:12]))
            pairs.append((w_ref.at[a, 0:2, 2, 2], wv.at[a, 12]))
            pairs.append((w_ref.at[a, 2, 2, 2], wv.at[a, 13, 0]))
            for n, (src, dst) in enumerate(pairs):
                copies.append(pltpu.make_async_copy(src, dst, w_sem.at[which, a, n]))
        return copies

    w1_copies, w2_copies = weight_copies(w1_ref, b1_ref, wv1, 0), weight_copies(w2_ref, b2_ref, wv2, 1)
    for copy in w1_copies:
        copy.start()
    for copy in w2_copies:
        copy.start()

    def exchange(src, src_f, src_r, dst, stage):
        made = []
        for n, (dt, dh, f, r, to_f, to_r, sends, receives) in enumerate(routes):
            f = slice(f.start + src_f, f.stop + src_f)
            r = slice(r.start + src_r, r.stop + src_r)
            copy = pltpu.make_async_remote_copy(
                src_ref=src.at[f, r],
                dst_ref=dst.at[to_f, to_r],
                send_sem=send_sem.at[stage, n],
                recv_sem=recv_sem.at[stage, n],
                device_id={"tm": jnp.minimum(tm + dt, peers_t - 1), "height": jnp.clip(height + dh, 0, peers_h - 1)},
                device_id_type=MESH,
            )
            made.append((copy, sends, receives))
        return made

    def start(made):
        for copy, sends, _ in made:
            pl.when(sends)(copy.start)

    def finish(made, which):
        for copy, sends, receives in made:
            if which == "recv":
                pl.when(receives)(copy.wait_recv)
            else:
                pl.when(sends)(copy.wait_send)

    pl.semaphore_wait(barrier, sum(sends.astype(jnp.int32) for _, _, _, _, _, _, sends, _ in routes))

    sent_x = exchange(x_ref, 0, 0, xbuf, 0)
    start(sent_x)

    for buf in (xbuf, gbuf):
        @pl.when(jnp.logical_not(earlier))
        def _():
            buf[0:2] = jnp.zeros((2, rows + 2, cols, chans), buf.dtype)

        @pl.when(jnp.logical_not(upper))
        def _():
            buf[:, 0:1] = jnp.zeros((frames + 2, 1, cols, chans), buf.dtype)

        @pl.when(jnp.logical_not(lower))
        def _():
            buf[:, rows + 1 : rows + 2] = jnp.zeros((frames + 2, 1, cols, chans), buf.dtype)

    for wv in (wv1, wv2):
        for a in range(3):
            wv[a, 13, 1] = jnp.zeros((lo_chans, chans), wv.dtype)

    def lay(stack, value, f0, r0):
        nf, nr = value.shape[:2]
        column = lax.broadcasted_iota(jnp.int32, value.shape, 2)
        turned = (
            jnp.where(column == 0, 0.0, pltpu.roll(value, 1, 2)),
            value,
            jnp.where(column == cols - 1, 0.0, pltpu.roll(value, cols - 1, 2)),
        )
        high = [v[..., :128].astype(stack.dtype) for v in turned]
        low = [v[..., 128:] for v in turned]
        low01 = jnp.concatenate([low[0], low[1]], -1).astype(stack.dtype)
        low2 = jnp.concatenate([low[2], jnp.zeros_like(low[2])], -1).astype(stack.dtype)
        low2_right = jnp.concatenate([jnp.zeros_like(low[2]), low[2]], -1).astype(stack.dtype)
        for b in range(3):
            begin, end = max(r0 - b, 0), min(r0 + nr - b, rows)
            if begin >= end:
                continue
            source = slice(begin + b - r0, end + b - r0)
            target = (slice(f0, f0 + nf), slice(begin, end), slice(None))
            for e in range(3):
                stack[target + (slice((3 * b + e) * 128, (3 * b + e + 1) * 128),)] = high[e][:, source]
            stack[target + (slice(1152 + b * 128, 1280 + b * 128),)] = low01[:, source]
            if b == 0:
                stack[target + (slice(1536, 1536 + lo_chans),)] = low2[:, source][..., :lo_chans]
            elif b == 1:
                stack[target + (slice(1536 + lo_chans, 1664),)] = low2_right[:, source][..., lo_chans:]
            else:
                stack[target + (slice(1664, 1792),)] = low2[:, source]

    def lay_halo(stack, buf, fn):
        for f in range(2):
            lay(stack, fn(buf[f : f + 1].astype(jnp.float32)), f, 0)
        lay(stack, fn(buf[2 : frames + 2, 0:1].astype(jnp.float32)), 2, 0)
        lay(stack, fn(buf[2 : frames + 2, rows + 1 : rows + 2].astype(jnp.float32)), 2, rows + 1)

    def conv(stack, wv):
        left = jnp.concatenate([stack[a : a + frames].reshape(positions, depth) for a in range(3)], -1)
        return jnp.dot(left, wv[...].reshape(3 * depth, chans), preferred_element_type=jnp.float32)

    local_x.wait()
    for f in range(2, frames + 2):
        lay(stack1, silu(xbuf[f : f + 1, 1 : rows + 1].astype(jnp.float32)), f, 1)
    finish(sent_x, "recv")
    lay_halo(stack1, xbuf, silu)
    for copy in w1_copies:
        copy.wait()
    gated = silu(conv(stack1, wv1) + bias[0]).astype(jnp.bfloat16)
    gbuf[2 : frames + 2, 1 : rows + 1] = gated.reshape(frames, rows, cols, chans)

    sent_g = exchange(gbuf, 2, 1, gbuf, 1)
    start(sent_g)
    for f in range(2, frames + 2):
        lay(stack2, gbuf[f : f + 1, 1 : rows + 1].astype(jnp.float32), f, 1)
    for copy in w2_copies:
        copy.wait()
    finish(sent_g, "recv")
    lay_halo(stack2, gbuf, lambda v: v)
    total = conv(stack2, wv2) + bias[1]
    own = xbuf[2 : frames + 2, 1 : rows + 1].astype(jnp.float32)
    out_ref[...] = (own + total.reshape(frames, rows, cols, chans)).astype(out_ref.dtype)
    finish(sent_x, "send")
    finish(sent_g, "send")


def local(peers_t, peers_h, clip_frames, w_first, b_first, w_second, b_second):
    frames, rows, cols, chans = clip_frames.shape
    kind = clip_frames.dtype
    parts = chans // 64
    padded = (frames + 2, rows + 2, cols, chans)
    stacked = (frames + 2, rows, cols, 14 * 128)
    weights = (3, 14, 2, 64, chans)
    anywhere, vmem = pl.BlockSpec(memory_space=pltpu.HBM), pl.BlockSpec(memory_space=pltpu.VMEM)
    return pl.pallas_call(
        functools.partial(kernel, peers_t, peers_h),
        out_shape=jax.ShapeDtypeStruct(clip_frames.shape, kind),
        in_specs=[anywhere] * 5,
        out_specs=vmem,
        scratch_shapes=[
            pltpu.VMEM(padded, kind),
            pltpu.VMEM(padded, kind),
            pltpu.VMEM(stacked, kind),
            pltpu.VMEM(stacked, kind),
            pltpu.VMEM(weights, kind),
            pltpu.VMEM(weights, kind),
            pltpu.VMEM((2, 1, chans), jnp.float32),
            pltpu.SemaphoreType.DMA,
            pltpu.SemaphoreType.DMA((2,)),
            pltpu.SemaphoreType.DMA((2, 3, 6)),
            pltpu.SemaphoreType.DMA((2, 5)),
            pltpu.SemaphoreType.DMA((2, 5)),
        ],
        compiler_params=pltpu.CompilerParams(
            collective_id=0, has_side_effects=True, vmem_limit_bytes=61 * 1024 * 1024
        ),
    )(
        clip_frames,
        w_first.reshape(3, 3, 3, parts, 64, chans),
        b_first.reshape(1, chans),
        w_second.reshape(3, 3, 3, parts, 64, chans),
        b_second.reshape(1, chans),
    )


def solution(mesh):
    return jax.shard_map(
        functools.partial(local, mesh.shape["tm"], mesh.shape["height"]),
        mesh=mesh,
        in_specs=(P(("clips", "tm"), "height", None, None), P(), P(), P(), P()),
        out_specs=P(("clips", "tm"), "height", None, None),
        check_vma=False,
    )
```

```python
import functools

import jax
import jax.numpy as jnp
from jax import lax
from jax.experimental import pallas as pl
from jax.experimental.pallas import tpu as pltpu
from jax.sharding import PartitionSpec as P

MESH = pl.DeviceIdType.MESH


def silu(v):
    return 0.5 * v * (1.0 + jnp.tanh(0.5 * v))


def kernel(
    peers_t, peers_h, x_ref, w1_ref, b1_ref, w2_ref, b2_ref, out_ref,
    xbuf, gbuf, stack1, stack2, wv1, wv2, bias, x_sem, b_sem, w_sem, send_sem, recv_sem,
):
    frames, rows, cols, chans = x_ref.shape
    lo_chans = chans - 128
    positions = frames * rows * cols
    depth = stack1.shape[-1]
    tm, height = lax.axis_index("tm"), lax.axis_index("height")
    later, lower, upper = tm < peers_t - 1, height < peers_h - 1, height > 0
    earlier = tm > 0

    every, tail, before = slice(2, frames + 2), slice(frames, frames + 2), slice(0, 2)
    body, first, last = slice(1, rows + 1), slice(1, 2), slice(rows, rows + 1)
    above, below = slice(0, 1), slice(rows + 1, rows + 2)
    own_f, own_r = every, body

    def rows_of(f):
        return (
            (0, 1, f, last, f, above, lower, upper),
            (0, -1, f, first, f, below, upper, lower),
        )

    onward = (
        (1, 0, tail, body, before, body, later, earlier),
        (1, 1, tail, last, before, above, later & lower, earlier & upper),
        (1, -1, tail, first, before, below, later & upper, earlier & lower),
    )
    routes = rows_of(every) + onward

    barrier = pltpu.get_barrier_semaphore()
    for dt, dh, _, _, _, _, _, receives in routes:
        @pl.when(receives)
        def _():
            pl.semaphore_signal(
                barrier, inc=1,
                device_id={"tm": jnp.maximum(tm - dt, 0), "height": jnp.clip(height - dh, 0, peers_h - 1)},
                device_id_type=MESH,
            )

    local_x = pltpu.make_async_copy(x_ref, xbuf.at[own_f, own_r], x_sem)
    local_x.start()

    def weight_copies(w_ref, b_ref, wv, which):
        copies = [pltpu.make_async_copy(b_ref, bias.at[which], b_sem.at[which])]
        for a in range(3):
            pairs = [(w_ref.at[a, b, :, 0:2], wv.at[a, 3 * b : 3 * b + 3]) for b in range(3)]
            pairs.append((w_ref.at[a, :, 0:2, 2], wv.at[a, 9:12]))
            pairs.append((w_ref.at[a, 0:2, 2, 2], wv.at[a, 12]))
            pairs.append((w_ref.at[a, 2, 2, 2], wv.at[a, 13, 0]))
            for n, (src, dst) in enumerate(pairs):
                copies.append(pltpu.make_async_copy(src, dst, w_sem.at[which, a, n]))
        return copies

    w1_copies, w2_copies = weight_copies(w1_ref, b1_ref, wv1, 0), weight_copies(w2_ref, b2_ref, wv2, 1)
    for copy in w1_copies:
        copy.start()
    def exchange(src, base_f, base_r, dst, plan, stage, sem):
        made = []
        for n, (dt, dh, f, r, to_f, to_r, sends, receives) in enumerate(plan, sem):
            f = slice(f.start - base_f, f.stop - base_f)
            r = slice(r.start - base_r, r.stop - base_r)
            copy = pltpu.make_async_remote_copy(
                src_ref=src.at[f, r],
                dst_ref=dst.at[to_f, to_r],
                send_sem=send_sem.at[stage, n],
                recv_sem=recv_sem.at[stage, n],
                device_id={"tm": jnp.minimum(tm + dt, peers_t - 1), "height": jnp.clip(height + dh, 0, peers_h - 1)},
                device_id_type=MESH,
            )
            made.append((copy, sends, receives))
        return made

    def start(made):
        for copy, sends, _ in made:
            pl.when(sends)(copy.start)

    def finish(made, which):
        for copy, sends, receives in made:
            if which == "recv":
                pl.when(receives)(copy.wait_recv)
            else:
                pl.when(sends)(copy.wait_send)

    pl.semaphore_wait(barrier, sum(sends.astype(jnp.int32) for _, _, _, _, _, _, sends, _ in routes))

    sent_x = exchange(x_ref, 2, 1, xbuf, routes, 0, 0)
    start(sent_x)
    for copy in w2_copies:
        copy.start()

    for buf in (xbuf, gbuf):
        @pl.when(jnp.logical_not(earlier))
        def _():
            buf[0:2] = jnp.zeros((2, rows + 2, cols, chans), buf.dtype)

        @pl.when(jnp.logical_not(upper))
        def _():
            buf[:, 0:1] = jnp.zeros((frames + 2, 1, cols, chans), buf.dtype)

        @pl.when(jnp.logical_not(lower))
        def _():
            buf[:, rows + 1 : rows + 2] = jnp.zeros((frames + 2, 1, cols, chans), buf.dtype)

    for wv in (wv1, wv2):
        for a in range(3):
            wv[a, 13, 1] = jnp.zeros((lo_chans, chans), wv.dtype)

    def lay(stack, value, f0, r0):
        nf, nr = value.shape[:2]
        column = lax.broadcasted_iota(jnp.int32, value.shape, 2)
        turned = (
            jnp.where(column == 0, 0.0, pltpu.roll(value, 1, 2)),
            value,
            jnp.where(column == cols - 1, 0.0, pltpu.roll(value, cols - 1, 2)),
        )
        high = [v[..., :128].astype(stack.dtype) for v in turned]
        low = [v[..., 128:] for v in turned]
        low01 = jnp.concatenate([low[0], low[1]], -1).astype(stack.dtype)
        low2 = jnp.concatenate([low[2], jnp.zeros_like(low[2])], -1).astype(stack.dtype)
        low2_right = jnp.concatenate([jnp.zeros_like(low[2]), low[2]], -1).astype(stack.dtype)
        for b in range(3):
            begin, end = max(r0 - b, 0), min(r0 + nr - b, rows)
            if begin >= end:
                continue
            source = slice(begin + b - r0, end + b - r0)
            target = (slice(f0, f0 + nf), slice(begin, end), slice(None))
            for e in range(3):
                stack[target + (slice((3 * b + e) * 128, (3 * b + e + 1) * 128),)] = high[e][:, source]
            stack[target + (slice(1152 + b * 128, 1280 + b * 128),)] = low01[:, source]
            if b == 0:
                stack[target + (slice(1536, 1536 + lo_chans),)] = low2[:, source][..., :lo_chans]
            elif b == 1:
                stack[target + (slice(1536 + lo_chans, 1664),)] = low2_right[:, source][..., lo_chans:]
            else:
                stack[target + (slice(1664, 1792),)] = low2[:, source]

    def lay_rows(stack, buf, fn, f):
        lay(stack, fn(buf[f, 0:1].astype(jnp.float32)), f.start, 0)
        lay(stack, fn(buf[f, rows + 1 : rows + 2].astype(jnp.float32)), f.start, rows + 1)

    def lay_before(stack, buf, fn):
        for f in range(2):
            lay(stack, fn(buf[f : f + 1].astype(jnp.float32)), f, 0)

    def conv(stack, wv, pieces):
        left = jnp.concatenate(
            [
                jnp.concatenate(
                    [
                        stack[a + f.start : a + f.stop, r].reshape((f.stop - f.start) * (r.stop - r.start) * cols, depth)
                        for f, r in pieces
                    ],
                    0,
                )
                for a in range(3)
            ],
            -1,
        )
        return jnp.dot(left, wv[...].reshape(3 * depth, chans), preferred_element_type=jnp.float32)

    def gate(f):
        total = conv(stack1, wv1, [(f, slice(0, rows))])
        gated = silu(total + bias[0]).astype(gbuf.dtype).reshape(f.stop - f.start, rows, cols, chans)
        gbuf[f.start + 2 : f.stop + 2, 1 : rows + 1] = gated
        return gated.astype(jnp.float32)

    def finish_block(pieces):
        total = conv(stack2, wv2, pieces) + bias[1]
        begin = 0
        for f, r in pieces:
            nf, nr = f.stop - f.start, r.stop - r.start
            part = total[begin : begin + nf * nr * cols].reshape(nf, nr, cols, chans)
            begin += nf * nr * cols
            own = xbuf[f.start + 2 : f.stop + 2, r.start + 1 : r.stop + 1].astype(jnp.float32)
            out_ref[f, r] = (own + part).astype(out_ref.dtype)

    local_x.wait()
    for f in range(2, frames + 2):
        lay(stack1, silu(xbuf[f : f + 1, 1 : rows + 1].astype(jnp.float32)), f, 1)
    for copy in w1_copies:
        copy.wait()
    finish(sent_x[:2], "recv")
    lay_rows(stack1, xbuf, silu, every)

    late, soon = slice(2, frames), slice(0, 2)
    gated = gate(late)
    sent_g = exchange(gbuf, 0, 0, gbuf, onward + rows_of(slice(4, frames + 2)), 1, 0)
    start(sent_g)
    lay(stack2, gated, 4, 1)
    finish(sent_x[2:], "recv")
    lay_before(stack1, xbuf, silu)
    gated = gate(soon)
    sent_rows = exchange(gbuf, 0, 0, gbuf, rows_of(slice(2, 4)), 1, 5)
    start(sent_rows)
    lay(stack2, gated, 2, 1)
    for copy in w2_copies:
        copy.wait()
    finish_block([(late, slice(1, rows - 1))])
    finish(sent_g, "recv")
    finish(sent_rows, "recv")
    lay_rows(stack2, gbuf, lambda v: v, every)
    lay_before(stack2, gbuf, lambda v: v)
    finish_block([(soon, slice(0, rows)), (late, slice(0, 1)), (late, slice(rows - 1, rows))])
    finish(sent_x, "send")
    finish(sent_g, "send")
    finish(sent_rows, "send")


def local(peers_t, peers_h, clip_frames, w_first, b_first, w_second, b_second):
    frames, rows, cols, chans = clip_frames.shape
    kind = clip_frames.dtype
    parts = chans // 64
    padded = (frames + 2, rows + 2, cols, chans)
    stacked = (frames + 2, rows, cols, 14 * 128)
    weights = (3, 14, 2, 64, chans)
    anywhere, vmem = pl.BlockSpec(memory_space=pltpu.HBM), pl.BlockSpec(memory_space=pltpu.VMEM)
    return pl.pallas_call(
        functools.partial(kernel, peers_t, peers_h),
        out_shape=jax.ShapeDtypeStruct(clip_frames.shape, kind),
        in_specs=[anywhere] * 5,
        out_specs=vmem,
        scratch_shapes=[
            pltpu.VMEM(padded, kind),
            pltpu.VMEM(padded, kind),
            pltpu.VMEM(stacked, kind),
            pltpu.VMEM(stacked, kind),
            pltpu.VMEM(weights, kind),
            pltpu.VMEM(weights, kind),
            pltpu.VMEM((2, 1, chans), jnp.float32),
            pltpu.SemaphoreType.DMA,
            pltpu.SemaphoreType.DMA((2,)),
            pltpu.SemaphoreType.DMA((2, 3, 6)),
            pltpu.SemaphoreType.DMA((2, 7)),
            pltpu.SemaphoreType.DMA((2, 7)),
        ],
        compiler_params=pltpu.CompilerParams(
            collective_id=0, has_side_effects=True, vmem_limit_bytes=61 * 1024 * 1024
        ),
    )(
        clip_frames,
        w_first.reshape(3, 3, 3, parts, 64, chans),
        b_first.reshape(1, chans),
        w_second.reshape(3, 3, 3, parts, 64, chans),
        b_second.reshape(1, chans),
    )


def solution(mesh):
    return jax.shard_map(
        functools.partial(local, mesh.shape["tm"], mesh.shape["height"]),
        mesh=mesh,
        in_specs=(P(("clips", "tm"), "height", None, None), P(), P(), P(), P()),
        out_specs=P(("clips", "tm"), "height", None, None),
        check_vma=False,
    )
```

```python
import functools

import jax
import jax.numpy as jnp
from jax import lax
from jax.experimental import pallas as pl
from jax.experimental.pallas import tpu as pltpu
from jax.sharding import PartitionSpec as P

MESH = pl.DeviceIdType.MESH


def silu(v):
    return 0.5 * v * (1.0 + jnp.tanh(0.5 * v))


def kernel(
    peers_t, peers_h, x_ref, w1_ref, b1_ref, w2_ref, b2_ref, out_ref,
    xbuf, gbuf, stack1, stack2, wv1, wv2, bias, x_sem, b_sem, w_sem, send_sem, recv_sem,
):
    frames, rows, cols, chans = x_ref.shape
    lo_chans = chans - 128
    positions = frames * rows * cols
    depth = stack1.shape[-1]
    tm, height = lax.axis_index("tm"), lax.axis_index("height")
    later, lower, upper = tm < peers_t - 1, height < peers_h - 1, height > 0
    earlier = tm > 0

    every, tail, before = slice(2, frames + 2), slice(frames, frames + 2), slice(0, 2)
    body, first, last = slice(1, rows + 1), slice(1, 2), slice(rows, rows + 1)
    above, below = slice(0, 1), slice(rows + 1, rows + 2)
    own_f, own_r = every, body

    def rows_of(f):
        return (
            (0, 1, f, last, f, above, lower, upper),
            (0, -1, f, first, f, below, upper, lower),
        )

    onward = (
        (1, 0, tail, body, before, body, later, earlier),
        (1, 1, tail, last, before, above, later & lower, earlier & upper),
        (1, -1, tail, first, before, below, later & upper, earlier & lower),
    )
    routes = rows_of(every) + onward

    barrier = pltpu.get_barrier_semaphore()
    for dt, dh, _, _, _, _, _, receives in routes:
        @pl.when(receives)
        def _():
            pl.semaphore_signal(
                barrier, inc=1,
                device_id={"tm": jnp.maximum(tm - dt, 0), "height": jnp.clip(height - dh, 0, peers_h - 1)},
                device_id_type=MESH,
            )

    local_x = pltpu.make_async_copy(x_ref, xbuf.at[own_f, own_r], x_sem)
    local_x.start()

    def weight_copies(w_ref, b_ref, wv, which):
        copies = [pltpu.make_async_copy(b_ref, bias.at[which], b_sem.at[which])]
        for a in range(3):
            pairs = [(w_ref.at[a, b, :, 0:2], wv.at[a, 3 * b : 3 * b + 3]) for b in range(3)]
            pairs.append((w_ref.at[a, :, 0:2, 2], wv.at[a, 9:12]))
            pairs.append((w_ref.at[a, 0:2, 2, 2], wv.at[a, 12]))
            pairs.append((w_ref.at[a, 2, 2, 2], wv.at[a, 13, 0]))
            for n, (src, dst) in enumerate(pairs):
                copies.append(pltpu.make_async_copy(src, dst, w_sem.at[which, a, n]))
        return copies

    w1_copies, w2_copies = weight_copies(w1_ref, b1_ref, wv1, 0), weight_copies(w2_ref, b2_ref, wv2, 1)
    for copy in w1_copies:
        copy.start()
    def exchange(src, base_f, base_r, dst, plan, stage, sem):
        made = []
        for n, (dt, dh, f, r, to_f, to_r, sends, receives) in enumerate(plan, sem):
            f = slice(f.start - base_f, f.stop - base_f)
            r = slice(r.start - base_r, r.stop - base_r)
            copy = pltpu.make_async_remote_copy(
                src_ref=src.at[f, r],
                dst_ref=dst.at[to_f, to_r],
                send_sem=send_sem.at[stage, n],
                recv_sem=recv_sem.at[stage, n],
                device_id={"tm": jnp.minimum(tm + dt, peers_t - 1), "height": jnp.clip(height + dh, 0, peers_h - 1)},
                device_id_type=MESH,
            )
            made.append((copy, sends, receives))
        return made

    def start(made):
        for copy, sends, _ in made:
            pl.when(sends)(copy.start)

    def finish(made, which):
        for copy, sends, receives in made:
            if which == "recv":
                pl.when(receives)(copy.wait_recv)
            else:
                pl.when(sends)(copy.wait_send)

    pl.semaphore_wait(barrier, sum(sends.astype(jnp.int32) for _, _, _, _, _, _, sends, _ in routes))

    sent_x = exchange(x_ref, 2, 1, xbuf, routes, 0, 0)
    start(sent_x)
    for copy in w2_copies:
        copy.start()

    for buf in (xbuf, gbuf):
        @pl.when(jnp.logical_not(earlier))
        def _():
            buf[0:2] = jnp.zeros((2, rows + 2, cols, chans), buf.dtype)

        @pl.when(jnp.logical_not(upper))
        def _():
            buf[:, 0:1] = jnp.zeros((frames + 2, 1, cols, chans), buf.dtype)

        @pl.when(jnp.logical_not(lower))
        def _():
            buf[:, rows + 1 : rows + 2] = jnp.zeros((frames + 2, 1, cols, chans), buf.dtype)

    for wv in (wv1, wv2):
        for a in range(3):
            wv[a, 13, 1] = jnp.zeros((lo_chans, chans), wv.dtype)

    def lay(stack, value, f0, r0):
        nf, nr = value.shape[:2]
        column = lax.broadcasted_iota(jnp.int32, value.shape, 2)
        turned = (
            jnp.where(column == 0, 0.0, pltpu.roll(value, 1, 2)),
            value,
            jnp.where(column == cols - 1, 0.0, pltpu.roll(value, cols - 1, 2)),
        )
        high = [v[..., :128].astype(stack.dtype) for v in turned]
        low = [v[..., 128:] for v in turned]
        low01 = jnp.concatenate([low[0], low[1]], -1).astype(stack.dtype)
        low2 = jnp.concatenate([low[2], jnp.zeros_like(low[2])], -1).astype(stack.dtype)
        low2_right = jnp.concatenate([jnp.zeros_like(low[2]), low[2]], -1).astype(stack.dtype)
        for b in range(3):
            begin, end = max(r0 - b, 0), min(r0 + nr - b, rows)
            if begin >= end:
                continue
            source = slice(begin + b - r0, end + b - r0)
            target = (slice(f0, f0 + nf), slice(begin, end), slice(None))
            for e in range(3):
                stack[target + (slice((3 * b + e) * 128, (3 * b + e + 1) * 128),)] = high[e][:, source]
            stack[target + (slice(1152 + b * 128, 1280 + b * 128),)] = low01[:, source]
            if b == 0:
                stack[target + (slice(1536, 1536 + lo_chans),)] = low2[:, source][..., :lo_chans]
            elif b == 1:
                stack[target + (slice(1536 + lo_chans, 1664),)] = low2_right[:, source][..., lo_chans:]
            else:
                stack[target + (slice(1664, 1792),)] = low2[:, source]

    def lay_rows(stack, buf, fn, f):
        lay(stack, fn(buf[f, 0:1].astype(jnp.float32)), f.start, 0)
        lay(stack, fn(buf[f, rows + 1 : rows + 2].astype(jnp.float32)), f.start, rows + 1)

    def lay_before(stack, buf, fn):
        for f in range(2):
            lay(stack, fn(buf[f : f + 1].astype(jnp.float32)), f, 0)

    def conv(stack, wv, pieces):
        left = jnp.concatenate(
            [
                jnp.concatenate(
                    [
                        stack[a + f.start : a + f.stop, r].reshape((f.stop - f.start) * (r.stop - r.start) * cols, depth)
                        for f, r in pieces
                    ],
                    0,
                )
                for a in range(3)
            ],
            -1,
        )
        return jnp.dot(left, wv[...].reshape(3 * depth, chans), preferred_element_type=jnp.float32)

    def gate(pieces):
        gated = silu(conv(stack1, wv1, pieces) + bias[0]).astype(gbuf.dtype)
        made, begin = [], 0
        for f, r in pieces:
            nf, nr = f.stop - f.start, r.stop - r.start
            part = gated[begin : begin + nf * nr * cols].reshape(nf, nr, cols, chans)
            begin += nf * nr * cols
            gbuf[f.start + 2 : f.stop + 2, r.start + 1 : r.stop + 1] = part
            made.append((part.astype(jnp.float32), f.start + 2, r.start + 1))
        return made

    def lay_own(made):
        for value, f0, r0 in made:
            lay(stack2, value, f0, r0)

    def finish_block(pieces):
        total = conv(stack2, wv2, pieces) + bias[1]
        begin = 0
        for f, r in pieces:
            nf, nr = f.stop - f.start, r.stop - r.start
            part = total[begin : begin + nf * nr * cols].reshape(nf, nr, cols, chans)
            begin += nf * nr * cols
            own = xbuf[f.start + 2 : f.stop + 2, r.start + 1 : r.stop + 1].astype(jnp.float32)
            out_ref[f, r] = (own + part).astype(out_ref.dtype)

    local_x.wait()
    for f in range(2, frames + 2):
        lay(stack1, silu(xbuf[f : f + 1, 1 : rows + 1].astype(jnp.float32)), f, 1)
    for copy in w1_copies:
        copy.wait()
    late, soon = slice(2, frames), slice(0, 2)
    inner = gate([(late, slice(1, rows - 1))])
    sent_inner = exchange(gbuf, 0, 0, gbuf, ((1, 0, tail, slice(2, rows), before, slice(2, rows), later, earlier),), 1, 0)
    start(sent_inner)
    finish(sent_x[:2], "recv")
    lay_rows(stack1, xbuf, silu, every)
    edges = gate([(late, slice(0, 1)), (late, slice(rows - 1, rows))])
    edge_routes = tuple((1, 0, tail, r, before, r, later, earlier) for r in (first, last))
    sent_g = exchange(gbuf, 0, 0, gbuf, edge_routes + onward[1:] + rows_of(slice(4, frames + 2)), 1, 1)
    start(sent_g)
    lay_own(inner + edges)
    finish(sent_x[2:], "recv")
    lay_before(stack1, xbuf, silu)
    gated = gate([(soon, slice(0, rows))])
    sent_rows = exchange(gbuf, 0, 0, gbuf, rows_of(slice(2, 4)), 1, 7)
    start(sent_rows)
    lay_own(gated)
    for copy in w2_copies:
        copy.wait()
    finish_block([(late, slice(1, rows - 1))])
    finish(sent_inner, "recv")
    finish(sent_g, "recv")
    finish(sent_rows, "recv")
    lay_rows(stack2, gbuf, lambda v: v, every)
    lay_before(stack2, gbuf, lambda v: v)
    finish_block([(soon, slice(0, rows)), (late, slice(0, 1)), (late, slice(rows - 1, rows))])
    finish(sent_x, "send")
    finish(sent_inner, "send")
    finish(sent_g, "send")
    finish(sent_rows, "send")


def local(peers_t, peers_h, clip_frames, w_first, b_first, w_second, b_second):
    frames, rows, cols, chans = clip_frames.shape
    kind = clip_frames.dtype
    parts = chans // 64
    padded = (frames + 2, rows + 2, cols, chans)
    stacked = (frames + 2, rows, cols, 14 * 128)
    weights = (3, 14, 2, 64, chans)
    anywhere, vmem = pl.BlockSpec(memory_space=pltpu.HBM), pl.BlockSpec(memory_space=pltpu.VMEM)
    return pl.pallas_call(
        functools.partial(kernel, peers_t, peers_h),
        out_shape=jax.ShapeDtypeStruct(clip_frames.shape, kind),
        in_specs=[anywhere] * 5,
        out_specs=vmem,
        scratch_shapes=[
            pltpu.VMEM(padded, kind),
            pltpu.VMEM(padded, kind),
            pltpu.VMEM(stacked, kind),
            pltpu.VMEM(stacked, kind),
            pltpu.VMEM(weights, kind),
            pltpu.VMEM(weights, kind),
            pltpu.VMEM((2, 1, chans), jnp.float32),
            pltpu.SemaphoreType.DMA,
            pltpu.SemaphoreType.DMA((2,)),
            pltpu.SemaphoreType.DMA((2, 3, 6)),
            pltpu.SemaphoreType.DMA((2, 9)),
            pltpu.SemaphoreType.DMA((2, 9)),
        ],
        compiler_params=pltpu.CompilerParams(
            collective_id=0, has_side_effects=True, vmem_limit_bytes=61 * 1024 * 1024
        ),
    )(
        clip_frames,
        w_first.reshape(3, 3, 3, parts, 64, chans),
        b_first.reshape(1, chans),
        w_second.reshape(3, 3, 3, parts, 64, chans),
        b_second.reshape(1, chans),
    )


def solution(mesh):
    return jax.shard_map(
        functools.partial(local, mesh.shape["tm"], mesh.shape["height"]),
        mesh=mesh,
        in_specs=(P(("clips", "tm"), "height", None, None), P(), P(), P(), P()),
        out_specs=P(("clips", "tm"), "height", None, None),
        check_vma=False,
    )
```

```python
import functools

import jax
import jax.numpy as jnp
from jax import lax
from jax.experimental import pallas as pl
from jax.experimental.pallas import tpu as pltpu
from jax.sharding import PartitionSpec as P

MESH = pl.DeviceIdType.MESH


def silu(v):
    return 0.5 * v * (1.0 + jnp.tanh(0.5 * v))


def kernel(
    peers_t, peers_h, x_ref, w1_ref, b1_ref, w2_ref, b2_ref, out_ref,
    xbuf, gbuf, stack1, stack2, wv1, wv2, bias, x_sem, b_sem, w_sem, send_sem, recv_sem,
):
    frames, rows, cols, chans = x_ref.shape
    lo_chans = chans - 128
    positions = frames * rows * cols
    depth = stack1.shape[-1]
    tm, height = lax.axis_index("tm"), lax.axis_index("height")
    later, lower, upper = tm < peers_t - 1, height < peers_h - 1, height > 0
    earlier = tm > 0

    every, tail, before = slice(2, frames + 2), slice(frames, frames + 2), slice(0, 2)
    body, first, last = slice(1, rows + 1), slice(1, 2), slice(rows, rows + 1)
    above, below = slice(0, 1), slice(rows + 1, rows + 2)
    own_f, own_r = every, body

    def rows_of(f):
        return (
            (0, 1, f, last, f, above, lower, upper),
            (0, -1, f, first, f, below, upper, lower),
        )

    onward = (
        (1, 0, tail, body, before, body, later, earlier),
        (1, 1, tail, last, before, above, later & lower, earlier & upper),
        (1, -1, tail, first, before, below, later & upper, earlier & lower),
    )
    routes = rows_of(every) + onward

    barrier = pltpu.get_barrier_semaphore()
    for dt, dh, _, _, _, _, _, receives in routes:
        @pl.when(receives)
        def _():
            pl.semaphore_signal(
                barrier, inc=1,
                device_id={"tm": jnp.maximum(tm - dt, 0), "height": jnp.clip(height - dh, 0, peers_h - 1)},
                device_id_type=MESH,
            )

    local_x = pltpu.make_async_copy(x_ref, xbuf.at[own_f, own_r], x_sem)
    local_x.start()

    def weight_copies(w_ref, b_ref, wv, which):
        copies = [pltpu.make_async_copy(b_ref, bias.at[which], b_sem.at[which])]
        for a in range(3):
            pairs = [(w_ref.at[a, b, :, 0:2], wv.at[a, 3 * b : 3 * b + 3]) for b in range(3)]
            pairs.append((w_ref.at[a, :, 0:2, 2], wv.at[a, 9:12]))
            pairs.append((w_ref.at[a, 0:2, 2, 2], wv.at[a, 12]))
            pairs.append((w_ref.at[a, 2, 2, 2], wv.at[a, 13, 0]))
            for n, (src, dst) in enumerate(pairs):
                copies.append(pltpu.make_async_copy(src, dst, w_sem.at[which, a, n]))
        return copies

    w1_copies, w2_copies = weight_copies(w1_ref, b1_ref, wv1, 0), weight_copies(w2_ref, b2_ref, wv2, 1)
    for copy in w1_copies:
        copy.start()
    def exchange(src, base_f, base_r, dst, plan, stage, sem):
        made = []
        for n, (dt, dh, f, r, to_f, to_r, sends, receives) in enumerate(plan, sem):
            f = slice(f.start - base_f, f.stop - base_f)
            r = slice(r.start - base_r, r.stop - base_r)
            copy = pltpu.make_async_remote_copy(
                src_ref=src.at[f, r],
                dst_ref=dst.at[to_f, to_r],
                send_sem=send_sem.at[stage, n],
                recv_sem=recv_sem.at[stage, n],
                device_id={"tm": jnp.minimum(tm + dt, peers_t - 1), "height": jnp.clip(height + dh, 0, peers_h - 1)},
                device_id_type=MESH,
            )
            made.append((copy, sends, receives))
        return made

    def start(made):
        for copy, sends, _ in made:
            pl.when(sends)(copy.start)

    def finish(made, which):
        for copy, sends, receives in made:
            if which == "recv":
                pl.when(receives)(copy.wait_recv)
            else:
                pl.when(sends)(copy.wait_send)

    pl.semaphore_wait(barrier, sum(sends.astype(jnp.int32) for _, _, _, _, _, _, sends, _ in routes))

    sent_x = exchange(x_ref, 2, 1, xbuf, routes, 0, 0)
    start(sent_x)
    for copy in w2_copies:
        copy.start()

    for buf in (xbuf, gbuf):
        @pl.when(jnp.logical_not(earlier))
        def _():
            buf[0:2] = jnp.zeros((2, rows + 2, cols, chans), buf.dtype)

        @pl.when(jnp.logical_not(upper))
        def _():
            buf[:, 0:1] = jnp.zeros((frames + 2, 1, cols, chans), buf.dtype)

        @pl.when(jnp.logical_not(lower))
        def _():
            buf[:, rows + 1 : rows + 2] = jnp.zeros((frames + 2, 1, cols, chans), buf.dtype)

    for wv in (wv1, wv2):
        for a in range(3):
            wv[a, 13, 1] = jnp.zeros((lo_chans, chans), wv.dtype)

    def lay(stack, value, f0, r0):
        nf, nr = value.shape[:2]
        column = lax.broadcasted_iota(jnp.int32, value.shape, 2)
        turned = (
            jnp.where(column == 0, 0.0, pltpu.roll(value, 1, 2)),
            value,
            jnp.where(column == cols - 1, 0.0, pltpu.roll(value, cols - 1, 2)),
        )
        high = [v[..., :128].astype(stack.dtype) for v in turned]
        low = [v[..., 128:] for v in turned]
        low01 = jnp.concatenate([low[0], low[1]], -1).astype(stack.dtype)
        low2 = jnp.concatenate([low[2], jnp.zeros_like(low[2])], -1).astype(stack.dtype)
        low2_right = jnp.concatenate([jnp.zeros_like(low[2]), low[2]], -1).astype(stack.dtype)
        for b in range(3):
            begin, end = max(r0 - b, 0), min(r0 + nr - b, rows)
            if begin >= end:
                continue
            source = slice(begin + b - r0, end + b - r0)
            target = (slice(f0, f0 + nf), slice(begin, end), slice(None))
            for e in range(3):
                stack[target + (slice((3 * b + e) * 128, (3 * b + e + 1) * 128),)] = high[e][:, source]
            stack[target + (slice(1152 + b * 128, 1280 + b * 128),)] = low01[:, source]
            if b == 0:
                stack[target + (slice(1536, 1536 + lo_chans),)] = low2[:, source][..., :lo_chans]
            elif b == 1:
                stack[target + (slice(1536 + lo_chans, 1664),)] = low2_right[:, source][..., lo_chans:]
            else:
                stack[target + (slice(1664, 1792),)] = low2[:, source]

    def lay_rows(stack, buf, fn, f):
        lay(stack, fn(buf[f, 0:1].astype(jnp.float32)), f.start, 0)
        lay(stack, fn(buf[f, rows + 1 : rows + 2].astype(jnp.float32)), f.start, rows + 1)

    def lay_before(stack, buf, fn):
        for f in range(2):
            lay(stack, fn(buf[f : f + 1].astype(jnp.float32)), f, 0)

    def conv(stack, wv, pieces):
        left = jnp.concatenate(
            [
                jnp.concatenate(
                    [
                        stack[a + f.start : a + f.stop, r].reshape((f.stop - f.start) * (r.stop - r.start) * cols, depth)
                        for f, r in pieces
                    ],
                    0,
                )
                for a in range(3)
            ],
            -1,
        )
        return jnp.dot(left, wv[...].reshape(3 * depth, chans), preferred_element_type=jnp.float32)

    def gate(pieces):
        gated = silu(conv(stack1, wv1, pieces) + bias[0]).astype(gbuf.dtype)
        made, begin = [], 0
        for f, r in pieces:
            nf, nr = f.stop - f.start, r.stop - r.start
            part = gated[begin : begin + nf * nr * cols].reshape(nf, nr, cols, chans)
            begin += nf * nr * cols
            gbuf[f.start + 2 : f.stop + 2, r.start + 1 : r.stop + 1] = part
            made.append((part.astype(jnp.float32), f.start + 2, r.start + 1))
        return made

    def lay_own(made):
        for value, f0, r0 in made:
            lay(stack2, value, f0, r0)

    def finish_block(pieces):
        total = conv(stack2, wv2, pieces) + bias[1]
        begin = 0
        for f, r in pieces:
            nf, nr = f.stop - f.start, r.stop - r.start
            part = total[begin : begin + nf * nr * cols].reshape(nf, nr, cols, chans)
            begin += nf * nr * cols
            own = xbuf[f.start + 2 : f.stop + 2, r.start + 1 : r.stop + 1].astype(jnp.float32)
            out_ref[f, r] = (own + part).astype(out_ref.dtype)

    local_x.wait()
    for f in range(2, frames + 2):
        lay(stack1, silu(xbuf[f : f + 1, 1 : rows + 1].astype(jnp.float32)), f, 1)
    for copy in w1_copies:
        copy.wait()
    late, soon = slice(2, frames), slice(0, 2)
    inner = gate([(late, slice(1, rows - 1))])
    sent_inner = exchange(gbuf, 0, 0, gbuf, ((1, 0, tail, slice(2, rows), before, slice(2, rows), later, earlier),), 1, 0)
    start(sent_inner)
    finish(sent_x[:2], "recv")
    lay_rows(stack1, xbuf, silu, every)
    edges = gate([(late, slice(0, 1)), (late, slice(rows - 1, rows))])
    edge_routes = tuple((1, 0, tail, r, before, r, later, earlier) for r in (first, last))
    sent_g = exchange(gbuf, 0, 0, gbuf, edge_routes + onward[1:] + rows_of(slice(4, frames + 2)), 1, 1)
    start(sent_g)
    finish(sent_x[2:], "recv")
    lay_before(stack1, xbuf, silu)
    gated = gate([(soon, slice(0, rows))])
    sent_rows = exchange(gbuf, 0, 0, gbuf, rows_of(slice(2, 4)), 1, 7)
    start(sent_rows)
    lay_own(inner + edges + gated)
    for copy in w2_copies:
        copy.wait()
    finish_block([(late, slice(1, rows - 1))])
    finish(sent_inner, "recv")
    finish(sent_g, "recv")
    finish(sent_rows, "recv")
    lay_rows(stack2, gbuf, lambda v: v, every)
    lay_before(stack2, gbuf, lambda v: v)
    finish_block([(soon, slice(0, rows)), (late, slice(0, 1)), (late, slice(rows - 1, rows))])
    finish(sent_x, "send")
    finish(sent_inner, "send")
    finish(sent_g, "send")
    finish(sent_rows, "send")


def local(peers_t, peers_h, clip_frames, w_first, b_first, w_second, b_second):
    frames, rows, cols, chans = clip_frames.shape
    kind = clip_frames.dtype
    parts = chans // 64
    padded = (frames + 2, rows + 2, cols, chans)
    stacked = (frames + 2, rows, cols, 14 * 128)
    weights = (3, 14, 2, 64, chans)
    anywhere, vmem = pl.BlockSpec(memory_space=pltpu.HBM), pl.BlockSpec(memory_space=pltpu.VMEM)
    return pl.pallas_call(
        functools.partial(kernel, peers_t, peers_h),
        out_shape=jax.ShapeDtypeStruct(clip_frames.shape, kind),
        in_specs=[anywhere] * 5,
        out_specs=vmem,
        scratch_shapes=[
            pltpu.VMEM(padded, kind),
            pltpu.VMEM(padded, kind),
            pltpu.VMEM(stacked, kind),
            pltpu.VMEM(stacked, kind),
            pltpu.VMEM(weights, kind),
            pltpu.VMEM(weights, kind),
            pltpu.VMEM((2, 1, chans), jnp.float32),
            pltpu.SemaphoreType.DMA,
            pltpu.SemaphoreType.DMA((2,)),
            pltpu.SemaphoreType.DMA((2, 3, 6)),
            pltpu.SemaphoreType.DMA((2, 9)),
            pltpu.SemaphoreType.DMA((2, 9)),
        ],
        compiler_params=pltpu.CompilerParams(
            collective_id=0, has_side_effects=True, vmem_limit_bytes=61 * 1024 * 1024
        ),
    )(
        clip_frames,
        w_first.reshape(3, 3, 3, parts, 64, chans),
        b_first.reshape(1, chans),
        w_second.reshape(3, 3, 3, parts, 64, chans),
        b_second.reshape(1, chans),
    )


def solution(mesh):
    return jax.shard_map(
        functools.partial(local, mesh.shape["tm"], mesh.shape["height"]),
        mesh=mesh,
        in_specs=(P(("clips", "tm"), "height", None, None), P(), P(), P(), P()),
        out_specs=P(("clips", "tm"), "height", None, None),
        check_vma=False,
    )
```
